32 devices in a mesh: groups: 2 (over y), ctx: 4 (over z), head: 2 (over x), batch: 2 (over core).
Axes of the slice: x: 2, y: 2, z: 4, core: 2. Of those that a mesh axis runs over, the one named last changes fastest.
Arguments:
- queries: bfloat16 [4, 2048, 1024], P(('groups', 'batch'), 'ctx', 'head'), parts along dimension 0, may hold values from -200 to 200
- key_states: bfloat16 [4, 2048, 1024], P(('groups', 'batch'), 'ctx', 'head'), parts along dimension 0, may hold values from -16 to 16
- value_states: bfloat16 [4, 2048, 1024], P(('groups', 'batch'), 'ctx', 'head'), parts along dimension 0, may hold values from -16 to 16
- grad_out: bfloat16 [4, 2048, 1024], P(('groups', 'batch'), 'ctx'), parts along dimension 0, may hold values from -24 to 24
- out_weight: bfloat16 [1024, 1024], P('head'), may hold values from -0.1875 to 0.1875
Outputs:
- grad_queries: bfloat16 [4, 2048, 1024], P(('groups', 'batch'), 'ctx', 'head'), parts along dimension 0
- grad_keys: bfloat16 [4, 2048, 1024], P(('groups', 'batch'), 'ctx', 'head'), parts along dimension 0
- grad_values: bfloat16 [4, 2048, 1024], P(('groups', 'batch'), 'ctx', 'head'), parts along dimension 0
- grad_weight: float32 [2048, 1024], P(('groups', 'head')), parts along dimension 0
The draws below stay inside these ranges and needn't reach their ends.
There are 2 independent parts, one for each index of `groups`. The reference program is written for one: setup_inputs(seed, part) draws one part's arguments, and reference() takes and returns one part's arrays. A program takes and returns all parts, laid end to end along the dimension named above; an argument that names none is the same for every part. Nothing has to cross between parts.
All inputs are finite; a program needn't handle non-finite values.
Results may differ from the reference program's by a relative error of at most 0.02.
Values may be sent and summed in bfloat16 or wider, within the bound.
A program may use at most 128 MiB of HBM per device.

```python
import jax
import jax.numpy as jnp
from jax import lax

D = 1024
HEADS = 8
HEAD_DIM = 128
LEAF = 128
LENGTH = 2048
SEQS = 2


def layered(key):
    shape_all = (SEQS, LENGTH, HEADS * HEAD_DIM)
    rough = jnp.clip(jax.random.normal(jax.random.fold_in(key, 1), shape_all, jnp.float32), -4.0, 4.0)
    summed = 0.6 * rough
    scale_count = (LENGTH // LEAF).bit_length() - 1
    for level_num in range(scale_count):
        block_len = LEAF * 2 ** level_num
        piece_rows = jnp.clip(jax.random.normal(jax.random.fold_in(key, 10 + level_num), (SEQS, LENGTH // block_len, HEADS * HEAD_DIM), jnp.float32), -3.0, 3.0)
        summed = summed + 0.35 * jnp.repeat(piece_rows, block_len, axis=1)
    return summed


def paired_draw(key):
    key_base = layered(jax.random.fold_in(key, 101))
    query_base = layered(jax.random.fold_in(key, 202))
    return (query_base, key_base)


def draw_queries(key, part):
    return paired_draw(key)[0].astype(jnp.bfloat16)


def draw_key_states(key, part):
    return paired_draw(key)[1].astype(jnp.bfloat16)


def draw_value_states(key, part):
    return layered(jax.random.fold_in(key, 606)).astype(jnp.bfloat16)


def block_levels(rng, shape, shards, smallest, top_value):
    level, own = 1.0, jax.random.fold_in(rng, 6)
    for dim, blocks in shards:
        heights = jnp.exp(jax.random.uniform(jax.random.fold_in(own, dim), (blocks,), jnp.float32, smallest / len(shards), top_value / len(shards)))
        level = level * jnp.repeat(heights, shape[dim] // blocks).reshape([-1 if axis == dim else 1 for axis in range(len(shape))])
    return level


def bell_draw(own_key, shape, deviation, most, pieces=(), kind=jnp.bfloat16):
    gain = block_levels(own_key, shape, pieces, -0.22, 0.18) if pieces else 1.0
    values = jax.random.normal(own_key, shape, jnp.float32) * deviation * gain
    return jnp.minimum(jnp.maximum(values, -most), most).astype(kind)


def setup_inputs(seed: int = 0, part: int = 0) -> dict:
    streams_of = jax.random.split(jax.random.key(seed), 6)
    part_keys = jax.random.split(jax.random.fold_in(streams_of[5], part), 6)
    queries = draw_queries(jax.random.fold_in(jax.random.fold_in(streams_of[5], part), 71), part)
    key_states = draw_key_states(jax.random.fold_in(jax.random.fold_in(streams_of[5], part), 71), part)
    value_states = draw_value_states(jax.random.fold_in(jax.random.fold_in(streams_of[5], part), 71), part)
    grad_out = bell_draw(part_keys[3], (SEQS, LENGTH, D), 4.0, 24.0, ((0, 2), (1, 4)))
    out_weight = bell_draw(streams_of[4], (HEADS * HEAD_DIM, D), D ** -0.5, 0.1875, ((0, 2),))
    return {"queries": queries, "key_states": key_states, "value_states": value_states, "grad_out": grad_out, "out_weight": out_weight}


NEG_BIG = -1e30


def to_half(array_in):
    return array_in.astype(jnp.bfloat16)


def product(form, left, right):
    return jnp.einsum(form, left.astype(jnp.float32), right.astype(jnp.float32))


def pool_pairs(items):
    paired = items.reshape((items.shape[0] // 2, 2) + items.shape[1:]).astype(jnp.float32)
    return to_half((paired[:, 0] + paired[:, 1]) * 0.5)


def spread_half(grads):
    return jnp.repeat(grads * 0.5, 2, axis=0)


def swap_sibling(blocks_in):
    paired = blocks_in.reshape((blocks_in.shape[0] // 2, 2) + blocks_in.shape[1:])
    return paired[:, ::-1].reshape(blocks_in.shape)


def three_blocks(padded, blocks, leaf_rows):
    parts = []
    for offset in range(3):
        parts.append(padded[offset * leaf_rows: offset * leaf_rows + blocks * leaf_rows].reshape((blocks, leaf_rows) + padded.shape[1:]))
    return jnp.concatenate(parts, axis=1)


def fold_rims(grad3, blocks):
    leaf_rows = grad3.shape[1] // 3
    summed = 0.0
    for offset in range(3):
        piece_rows = grad3[:, offset * leaf_rows:(offset + 1) * leaf_rows].reshape((blocks * leaf_rows,) + grad3.shape[2:])
        pad_spec = ((offset * leaf_rows, (2 - offset) * leaf_rows),) + ((0, 0),) * (piece_rows.ndim - 1)
        summed = summed + jnp.pad(piece_rows, pad_spec)
    return summed


def forward_core(query_blocks, key_blocks, value_blocks, key_valid, terms, score_scale):
    blocks, leaf_rows, head_count, head_width = query_blocks.shape
    row_count = blocks * leaf_rows
    scores0 = product("bqhd,bkhd->bqhk", query_blocks, key_blocks) * score_scale
    scores0 = jnp.where(key_valid[:, None, None, :], scores0, NEG_BIG)
    fine_scores = []
    for coarse_q, coarse_k, coarse_v, factor in terms:
        coarse = product("nrhd,nkhd->nrhk", coarse_q, coarse_k) * score_scale
        fine_scores.append(jnp.repeat(coarse, factor, axis=1))
    highest = jnp.max(scores0, axis=3).reshape(row_count, head_count)
    for scores in fine_scores:
        highest = jnp.maximum(highest, jnp.max(scores, axis=3).reshape(row_count, head_count))
    probs0 = jnp.exp(scores0 - highest.reshape(blocks, leaf_rows, head_count)[..., None])
    totals = jnp.sum(probs0, axis=3).reshape(row_count, head_count)
    numerator = product("bqhk,bkhd->bqhd", to_half(probs0), value_blocks).reshape(row_count, head_count, head_width)
    weights_list = []
    for scores, level_term in zip(fine_scores, terms):
        block_count, fine_rows = scores.shape[0], scores.shape[1]
        weights = jnp.exp(scores - highest.reshape(block_count, fine_rows, head_count)[..., None])
        totals = totals + jnp.sum(weights, axis=3).reshape(row_count, head_count)
        numerator = numerator + product("nshk,nkhd->nshd", to_half(weights), level_term[2]).reshape(row_count, head_count, head_width)
        weights_list.append(weights)
    attended = to_half(numerator / totals[..., None])
    return attended, probs0, weights_list, totals


def backward_core(query_blocks, key_blocks, value_blocks, terms, grad_attn, attended, probs0, weights_list, totals, score_scale):
    blocks, leaf_rows, head_count, head_width = query_blocks.shape
    deltas = jnp.sum(grad_attn.astype(jnp.float32) * attended.astype(jnp.float32), axis=2)
    grad_blocks = grad_attn.reshape(blocks, leaf_rows, head_count, head_width)
    inner0 = product("bqhd,bkhd->bqhk", grad_blocks, value_blocks)
    normed0 = probs0 / totals.reshape(blocks, leaf_rows, head_count)[..., None]
    slopes0 = to_half(normed0 * (inner0 - deltas.reshape(blocks, leaf_rows, head_count)[..., None]) * score_scale)
    grad_q0 = product("bqhk,bkhd->bqhd", slopes0, key_blocks)
    grad_k3 = product("bqhk,bqhd->bkhd", slopes0, query_blocks)
    grad_v3 = product("bqhk,bqhd->bkhd", to_half(normed0), grad_blocks)
    level_grads = []
    for weights, level_term in zip(weights_list, terms):
        coarse_q, coarse_k, coarse_v, factor = level_term
        block_count, fine_rows = weights.shape[0], weights.shape[1]
        grad_fine = grad_attn.reshape(block_count, fine_rows, head_count, head_width)
        inner = product("nshd,nkhd->nshk", grad_fine, coarse_v)
        normed = weights / totals.reshape(block_count, fine_rows, head_count)[..., None]
        slopes = normed * (inner - deltas.reshape(block_count, fine_rows, head_count)[..., None])
        slopes = to_half(jnp.sum(slopes.reshape(block_count, fine_rows // factor, factor, head_count, -1), axis=2) * score_scale)
        level_grads.append((product("nrhk,nkhd->nrhd", slopes, coarse_k), product("nrhk,nrhd->nkhd", slopes, coarse_q), product("nshk,nshd->nkhd", to_half(normed), grad_fine)))
    return grad_q0, grad_k3, grad_v3, level_grads


def head_pass(query_head, key_head, value_head, grad_head):
    length_all, head_count, head_width = query_head.shape
    score_scale = head_width ** -0.5
    blocks = length_all // LEAF
    zero_rim = jnp.zeros((LEAF, head_count, head_width), jnp.bfloat16)
    key_blocks = three_blocks(jnp.concatenate([zero_rim, key_head, zero_rim]), blocks, LEAF)
    value_blocks = three_blocks(jnp.concatenate([zero_rim, value_head, zero_rim]), blocks, LEAF)
    position = jnp.arange(blocks)[:, None] * LEAF + jnp.arange(3 * LEAF)[None, :] - LEAF
    key_valid = (position >= 0) & (position < length_all)
    query_blocks = query_head.reshape(blocks, LEAF, head_count, head_width)
    terms = []
    q_level, k_level, v_level = query_head, key_head, value_head
    top_level = blocks.bit_length() - 2
    for level_num in range(1, top_level + 1):
        q_level = pool_pairs(q_level)
        k_level = pool_pairs(k_level)
        v_level = pool_pairs(v_level)
        block_count = q_level.shape[0] // LEAF
        shape_blocks = (block_count, LEAF, head_count, head_width)
        terms.append((q_level.reshape(shape_blocks), swap_sibling(k_level.reshape(shape_blocks)), swap_sibling(v_level.reshape(shape_blocks)), 2 ** level_num))
    attended, probs0, weights_list, totals = forward_core(query_blocks, key_blocks, value_blocks, key_valid, terms, score_scale)
    grad_q0, grad_k3, grad_v3, level_grads = backward_core(query_blocks, key_blocks, value_blocks, terms, grad_head, attended, probs0, weights_list, totals, score_scale)
    key_grad = fold_rims(grad_k3, blocks)[LEAF:LEAF + length_all]
    value_grad = fold_rims(grad_v3, blocks)[LEAF:LEAF + length_all]
    row_shape = (-1, head_count, head_width)
    q_chain = None
    k_chain = None
    v_chain = None
    for grad_qc, grad_kc, grad_vc in reversed(level_grads):
        q_rows = grad_qc.reshape(row_shape)
        k_rows = swap_sibling(grad_kc).reshape(row_shape)
        v_rows = swap_sibling(grad_vc).reshape(row_shape)
        if q_chain is None:
            q_chain, k_chain, v_chain = q_rows, k_rows, v_rows
        else:
            q_chain = q_rows + spread_half(q_chain)
            k_chain = k_rows + spread_half(k_chain)
            v_chain = v_rows + spread_half(v_chain)
    query_grad = grad_q0.reshape(length_all, head_count, head_width) + spread_half(q_chain)
    key_grad = key_grad + spread_half(k_chain)
    value_grad = value_grad + spread_half(v_chain)
    return attended, to_half(query_grad), to_half(key_grad), to_half(value_grad)


def reference(queries, key_states, value_states, grad_out, out_weight):
    seq_count, length_all, width_all = queries.shape
    head_width = HEAD_DIM
    heads_all = width_all // head_width
    weight_grad = jnp.zeros(out_weight.shape, jnp.float32)

    def split_heads(array_in):
        return array_in.reshape(length_all, heads_all, 1, head_width).transpose(1, 0, 2, 3)

    def join_heads(array_in):
        return array_in.transpose(1, 0, 2, 3).reshape(length_all, width_all)

    query_list = []
    key_list = []
    value_list = []
    for seq_num in range(seq_count):
        grad_attn = jnp.dot(grad_out[seq_num], out_weight.T, preferred_element_type=jnp.float32).astype(jnp.bfloat16)
        results = lax.map(lambda packed: head_pass(*packed), (split_heads(queries[seq_num]), split_heads(key_states[seq_num]), split_heads(value_states[seq_num]), split_heads(grad_attn)))
        attended = join_heads(results[0])
        weight_grad = weight_grad + jnp.dot(attended.T, grad_out[seq_num], preferred_element_type=jnp.float32)
        query_list.append(join_heads(results[1]))
        key_list.append(join_heads(results[2]))
        value_list.append(join_heads(results[3]))
    return jnp.stack(query_list), jnp.stack(key_list), jnp.stack(value_list), weight_grad
```

```python
import functools
import math

import jax
import jax.numpy as jnp
from jax import lax
from jax.experimental import pallas as pl
from jax.experimental.pallas import tpu as pltpu
from jax.sharding import PartitionSpec as P

HD = 128
LEAF = 128
NEG_BIG = -1e30
F32 = jnp.float32
BF16 = jnp.bfloat16


def nn(a, b):
    return lax.dot_general(a, b, (((1,), (0,)), ((), ())), preferred_element_type=F32)


def nt(a, b):
    return lax.dot_general(a, b, (((1,), (1,)), ((), ())), preferred_element_type=F32)


def tn(a, b):
    return lax.dot_general(a, b, (((0,), (0,)), ((), ())), preferred_element_type=F32)


def pool_matrix(rows, entry):
    r = lax.broadcasted_iota(jnp.int32, (rows, 2 * rows), 0)
    c = lax.broadcasted_iota(jnp.int32, (rows, 2 * rows), 1)
    return jnp.where((c == 2 * r) | (c == 2 * r + 1), entry, 0.0).astype(BF16)


def spread_matrix(rows, entry):
    r = lax.broadcasted_iota(jnp.int32, (2 * rows, rows), 0)
    c = lax.broadcasted_iota(jnp.int32, (2 * rows, rows), 1)
    return jnp.where((r == 2 * c) | (r == 2 * c + 1), entry, 0.0).astype(BF16)


def kernel(
    n, heads, rows,
    q_ref, k_ref, v_ref, go_ref, w_ref,
    dq_ref, dk_ref, dv_ref, gw_ref,
    kp, kv1, kvl, ql, ga, sib, attn, e0, g0, d0, el, gl, dl, fal, fbl,
    xa, xb, xc, dkp, dkv1, gout, gin, rout, rin, dql,
    wpart, wsend, wrecv, wacc, wrs, wfin,
    halo_s, halo_r, sib_s, sib_r, gs_s, gs_r, rim_s, rim_r, wp_s, wp_r, rs_s, rs_r, ag_s, ag_r, wf_s, wf_r,
):
    MESH = pl.DeviceIdType.MESH
    ctx = lax.axis_index("ctx")
    core = lax.axis_index("batch")
    other = 1 - core
    cross = n.bit_length() - 1
    wide = heads * HD
    blocks = rows // LEAF
    local = blocks.bit_length() - 1
    levels = list(range(1, local + cross))
    top = levels[-1]
    scale = HD ** (-0.5)
    c2 = scale * math.log2(math.e)

    def at(l):
        return sum(rows >> i for i in range(1, l))

    barrier = pltpu.get_barrier_semaphore()
    for m in range(1, n):
        pl.semaphore_signal(barrier, inc=1, device_id={"ctx": ctx ^ m}, device_id_type=MESH)
    pl.semaphore_signal(barrier, inc=1, device_id={"batch": other}, device_id_type=MESH)

    kp[LEAF : LEAF + rows, :wide] = k_ref[...]
    kp[LEAF : LEAF + rows, wide:] = v_ref[...]

    half = pool_matrix(LEAF, 0.5)

    def pool(x, cnt):
        return nn(half[: cnt, : 2 * cnt], x).astype(BF16)

    for b in range(blocks // 2):
        kv1[b * LEAF : (b + 1) * LEAF] = pool(kp[LEAF + 2 * b * LEAF : LEAF + 2 * (b + 1) * LEAF], LEAF)
    kv2 = pool(kv1[...], LEAF)
    for b in range(cross):
        cnt = LEAF >> b
        kvl[b, :cnt] = kv2
        if b + 1 < cross:
            kv2 = pool(kv2, cnt // 2)

    @pl.when(ctx == 0)
    def _():
        kp[:LEAF] = jnp.zeros((LEAF, 2 * wide), BF16)

    @pl.when(ctx == n - 1)
    def _():
        kp[LEAF + rows :] = jnp.zeros((LEAF, 2 * wide), BF16)

    pl.semaphore_wait(barrier, n)

    def remote(src, dst, s, r, **dev):
        return pltpu.make_async_remote_copy(
            src_ref=src, dst_ref=dst, send_sem=s, recv_sem=r, device_id=dev, device_id_type=MESH
        )

    right = jnp.minimum(ctx + 1, n - 1)
    left = jnp.maximum(ctx - 1, 0)
    to_right = remote(kp.at[pl.ds(rows, LEAF)], kp.at[pl.ds(0, LEAF)], halo_s.at[0], halo_r.at[0], ctx=right)
    to_left = remote(kp.at[pl.ds(LEAF, LEAF)], kp.at[pl.ds(rows + LEAF, LEAF)], halo_s.at[1], halo_r.at[1], ctx=left)

    has_right = ctx < n - 1
    has_left = ctx > 0

    def run_if(cond, fn):
        @pl.when(cond)
        def _():
            fn()

    def sib_copies(b):
        cnt = LEAF >> b
        mine = lax.rem(ctx, 1 << b) * cnt
        out = []
        for j in range(1 << b):
            peer = ctx ^ ((1 << b) | j)
            slot = (1 << b) - 1 + j
            out.append(remote(
                kvl.at[b, pl.ds(0, cnt)], sib.at[b, pl.ds(pl.multiple_of(mine, cnt), cnt)],
                sib_s.at[slot], sib_r.at[slot], ctx=peer))
        return out

    def sib_arrivals(b):
        cnt = LEAF >> b
        out = []
        for j in range(1 << b):
            peer = ctx ^ ((1 << b) | j)
            slot = (1 << b) - 1 + j
            theirs = lax.rem(peer, 1 << b) * cnt
            out.append(remote(
                kvl.at[b, pl.ds(0, cnt)], sib.at[b, pl.ds(pl.multiple_of(theirs, cnt), cnt)],
                sib_s.at[slot], sib_r.at[slot], ctx=peer))
        return out

    run_if(has_right, to_right.start)
    run_if(has_left, to_left.start)
    for b in range(cross):
        for c in sib_copies(b):
            c.start()

    for b in range(blocks // 2):
        ql[b * LEAF : (b + 1) * LEAF] = pool(q_ref[2 * b * LEAF : 2 * (b + 1) * LEAF], LEAF)
    for l in levels[1:]:
        cnt = rows >> l
        ql[at(l) : at(l) + cnt] = pool(ql[at(l - 1) : at(l - 1) + 2 * cnt], cnt)
    for b in range(blocks):
        ga[b * LEAF : (b + 1) * LEAF] = nt(go_ref[b * LEAF : (b + 1) * LEAF], w_ref[...]).astype(BF16)

    def coarse_keys(l):
        if l < local:
            return [
                (c * LEAF, LEAF, kv1, (c ^ 1) * LEAF) for c in range((rows >> l) // LEAF)
            ]
        return [(0, rows >> l, sib.at[l - local], 0)]

    def wide_row(x, cnt):
        return jnp.broadcast_to(x, (cnt, HD))

    def spread(ref, x, cnt):
        ref[pl.ds(0, cnt, stride=2), :] = x
        ref[pl.ds(1, cnt, stride=2), :] = x
        return ref[pl.ds(0, 2 * cnt), :]

    def gather_pairs(ref, x, cnt):
        ref[pl.ds(0, 2 * cnt), :] = x
        return ref[pl.ds(0, cnt, stride=2), :] + ref[pl.ds(1, cnt, stride=2), :]

    run_if(has_left, to_right.wait_recv)
    run_if(has_right, to_left.wait_recv)
    for b in range(cross):
        for c in sib_arrivals(b):
            c.wait_recv()

    def forward(h, carry):
        hs = pl.ds(pl.multiple_of(h * HD, HD), HD)
        vs = pl.ds(pl.multiple_of(wide + h * HD, HD), HD)
        acc = None
        for l in reversed(levels):
            parts = []
            for r0, cnt, ref, k0 in coarse_keys(l):
                s = nt(ql[at(l) + r0 : at(l) + r0 + cnt, hs], ref[k0 : k0 + LEAF, hs]) * c2
                m = wide_row(jnp.max(s, axis=1, keepdims=True), cnt)
                e = jnp.exp2(s - m)
                eb = e.astype(BF16)
                el[h, at(l) + r0 : at(l) + r0 + cnt] = eb
                parts.append((m, wide_row(jnp.sum(e, axis=1, keepdims=True), cnt), nn(eb, ref[k0 : k0 + LEAF, vs])))
            m, s, o = [jnp.concatenate(x) if len(x) > 1 else x[0] for x in zip(*parts)]
            cnt = rows >> l
            if acc is None:
                acc = (m, s, o)
                fal[at(l) : at(l) + cnt] = jnp.ones((cnt, HD), F32)
            else:
                am, as_, ao = [spread(r, x, cnt // 2) for r, x in zip((xa, xb, xc), acc)]
                nm = jnp.maximum(m, am)
                fa = jnp.exp2(m - nm)
                fb = jnp.exp2(am - nm)
                fal[at(l) : at(l) + cnt] = fa
                fbl[at(l) : at(l) + cnt] = fb
                acc = (nm, fa * s + fb * as_, fa * o + fb * ao)
        am, as_, ao = [spread(r, x, rows // 2) for r, x in zip((xa, xb, xc), acc)]
        mixed = []
        for b in range(blocks):
            br = slice(b * LEAF, (b + 1) * LEAF)
            kr = slice(b * LEAF, (b + 3) * LEAF)
            s = nt(q_ref[br, hs], kp[kr, hs]) * c2
            if b == 0:
                col = lax.broadcasted_iota(jnp.int32, s.shape, 1)
                s = jnp.where((col >= LEAF) | has_left, s, NEG_BIG)
            if b == blocks - 1:
                col = lax.broadcasted_iota(jnp.int32, s.shape, 1)
                s = jnp.where((col < 2 * LEAF) | has_right, s, NEG_BIG)
            m = wide_row(jnp.max(s, axis=1, keepdims=True), LEAF)
            e = jnp.exp2(s - jnp.concatenate([m, m, m], axis=1))
            eb = e.astype(BF16)
            e0[h, br] = eb
            su = wide_row(jnp.sum(e, axis=1, keepdims=True), LEAF)
            o = nn(eb, kp[kr, vs])
            nm = jnp.maximum(m, am[br])
            fa = jnp.exp2(m - nm)
            fb = jnp.exp2(am[br] - nm)
            inv = 1.0 / (fa * su + fb * as_[br])
            at_b = ((fa * o + fb * ao[br]) * inv).astype(BF16)
            attn[br, hs] = at_b
            af = at_b.astype(F32)
            g = ga[br, hs].astype(F32)
            gb = (g * (fa * inv)).astype(BF16)
            g0[br, hs] = gb
            d0[h, br] = wide_row(jnp.sum(gb.astype(F32) * af, axis=1, keepdims=True), LEAF)
            r1 = fb * inv
            mixed.append((g * r1, r1 * wide_row(jnp.sum(g * af, axis=1, keepdims=True), LEAF)))
        gc = jnp.concatenate([x[0] for x in mixed])
        dc = jnp.concatenate([x[1] for x in mixed])
        for l in levels:
            cnt = rows >> l
            gc = gather_pairs(xa, gc, cnt)
            dc = gather_pairs(xb, dc, cnt)
            fa = fal[at(l) : at(l) + cnt]
            gl[h, at(l) : at(l) + cnt] = (gc * fa).astype(BF16)
            dl[h, at(l) : at(l) + cnt] = dc * fa
            if l != top:
                fb = fbl[at(l) : at(l) + cnt]
                gc = gc * fb
                dc = dc * fb
        return carry

    lax.fori_loop(0, heads, forward, 0)

    wrow = wide // 2
    piece = wrow // n
    for b in range(wide // LEAF):
        hb = slice(b * LEAF, (b + 1) * LEAF)
        wpart[hb] = tn(attn[:, hb], go_ref[...])
    wsend[...] = wpart[pl.ds(pl.multiple_of(other * wrow, wrow), wrow)].astype(BF16)
    wp = remote(wsend, wrecv, wp_s, wp_r, batch=other)
    wp.start()

    def coarse_back(h, l):
        hs = pl.ds(pl.multiple_of(h * HD, HD), HD)
        vs = pl.ds(pl.multiple_of(wide + h * HD, HD), HD)
        for r0, cnt, ref, k0 in coarse_keys(l):
            r = slice(at(l) + r0, at(l) + r0 + cnt)
            keys = ref[k0 : k0 + LEAF, hs]
            eb = el[h, r]
            g = gl[h, r]
            inner = nt(g, ref[k0 : k0 + LEAF, vs])
            ds = (eb.astype(F32) * (inner - dl[h, r])).astype(BF16)
            dql[r, hs] = nn(ds, keys) * scale
            dk = tn(ds, ql[r, hs]) * scale
            dv = tn(eb, g)
            if l < local:
                dkv1[k0 : k0 + LEAF, hs] = dk
                dkv1[k0 : k0 + LEAF, vs] = dv
            else:
                gout[l - local, :, hs] = dk.astype(BF16)
                gout[l - local, :, vs] = dv.astype(BF16)

    def back_cross(h, carry):
        for l in levels[local - 1 :]:
            coarse_back(h, l)
        return carry

    lax.fori_loop(0, heads, back_cross, 0)

    def grad_copies(b):
        cnt = LEAF >> b
        out = []
        for j in range(1 << b):
            peer = ctx ^ ((1 << b) | j)
            slot = (1 << b) - 1 + j
            theirs = lax.rem(peer, 1 << b) * cnt
            out.append(remote(
                gout.at[b, pl.ds(pl.multiple_of(theirs, cnt), cnt)], gin.at[slot, pl.ds(0, cnt)],
                gs_s.at[slot], gs_r.at[slot], ctx=peer))
        return out

    for b in range(cross):
        for c in grad_copies(b):
            c.start()

    wp.wait()
    my_rows = pl.multiple_of(core * wrow, wrow)
    wacc[...] = (wpart[pl.ds(my_rows, wrow)] + wrecv[...].astype(F32)).astype(BF16)
    rs = []
    for m in range(1, n):
        peer = ctx ^ m
        c = remote(
            wacc.at[pl.ds(pl.multiple_of(peer * piece, piece), piece)], wrs.at[m - 1],
            rs_s.at[m - 1], rs_r.at[m - 1], ctx=peer)
        c.start()
        rs.append(c)

    dkp[...] = jnp.zeros_like(dkp)

    def back_level0(h, carry):
        hs = pl.ds(pl.multiple_of(h * HD, HD), HD)
        vs = pl.ds(pl.multiple_of(wide + h * HD, HD), HD)
        for b in range(blocks):
            br = slice(b * LEAF, (b + 1) * LEAF)
            kr = slice(b * LEAF, (b + 3) * LEAF)
            eb = e0[h, br]
            gb = g0[br, hs]
            keys = kp[kr, hs]
            d = d0[h, br]
            inner = nt(gb, kp[kr, vs])
            ds = (eb.astype(F32) * (inner - jnp.concatenate([d, d, d], axis=1))).astype(BF16)
            xc[br] = nn(ds, keys) * scale
            dkp[kr, hs] += tn(ds, q_ref[br, hs]) * scale
            dkp[kr, vs] += tn(eb, gb)
        for l in levels[: local - 1]:
            coarse_back(h, l)
        chain = None
        for l in reversed(levels):
            cnt = rows >> l
            x = dql[at(l) : at(l) + cnt, hs]
            if chain is not None:
                x = x + spread(xa, chain * 0.5, cnt // 2)
            chain = x
        dq_ref[:, hs] = (xc[...] + spread(xa, chain * 0.5, rows // 2)).astype(BF16)
        return carry

    lax.fori_loop(0, heads, back_level0, 0)

    rout[0] = dkp[:LEAF].astype(BF16)
    rout[1] = dkp[LEAF + rows :].astype(BF16)
    rim_left = remote(rout.at[0], rin.at[1], rim_s.at[0], rim_r.at[1], ctx=left)
    rim_right = remote(rout.at[1], rin.at[0], rim_s.at[1], rim_r.at[0], ctx=right)
    run_if(has_left, rim_left.start)
    run_if(has_right, rim_right.start)

    for c in rs:
        c.wait()
    mine = pl.multiple_of(ctx * piece, piece)
    tot = wacc[pl.ds(mine, piece)].astype(F32)
    for m in range(1, n):
        tot = tot + wrs[m - 1].astype(F32)
    wfin[core, pl.ds(mine, piece)] = tot.astype(BF16)
    ags = []
    for m in range(1, n):
        peer = ctx ^ m
        c = remote(
            wfin.at[core, pl.ds(mine, piece)], wfin.at[core, pl.ds(mine, piece)],
            ag_s.at[m - 1], ag_r.at[m - 1], ctx=peer)
        c.start()
        ags.append(c)

    for b in range(cross):
        for c in grad_copies(b):
            c.wait()
    twice = spread_matrix(LEAF, 0.5)

    def spread_wide(x, cnt):
        return nn(twice[: 2 * cnt, : cnt], x.astype(BF16))

    chain = None
    for b in reversed(range(cross)):
        cnt = LEAF >> b
        x = 0.0
        for j in range(1 << b):
            x = x + gin[(1 << b) - 1 + j, :cnt].astype(F32)
        if chain is not None:
            x = x + spread_wide(chain, cnt // 2)
        chain = x
    dkv1[...] += spread_wide(chain, LEAF)
    for b in range(blocks // 2):
        dkp[LEAF * (1 + 2 * b) : LEAF * (3 + 2 * b)] += spread_wide(dkv1[b * LEAF : (b + 1) * LEAF], LEAF)

    def left_arrival():
        rim_right.wait_recv()
        dkp[LEAF : 2 * LEAF] += rin[0].astype(F32)

    def right_arrival():
        rim_left.wait_recv()
        dkp[rows : rows + LEAF] += rin[1].astype(F32)

    run_if(has_left, left_arrival)
    run_if(has_right, right_arrival)
    dk_ref[...] = dkp[LEAF : LEAF + rows, :wide].astype(BF16)
    dv_ref[...] = dkp[LEAF : LEAF + rows, wide:].astype(BF16)

    for m in range(1, n):
        peer = ctx ^ m
        theirs = pl.multiple_of(peer * piece, piece)
        remote(
            wfin.at[core, pl.ds(mine, piece)], wfin.at[core, pl.ds(theirs, piece)],
            ag_s.at[m - 1], ag_r.at[m - 1], ctx=peer).wait_recv()
    for c in ags:
        c.wait_send()
    wf = remote(wfin.at[core], wfin.at[core], wf_s, wf_r, batch=other)
    wf.start()
    gw_ref[pl.ds(my_rows, wrow)] = wfin[core].astype(F32)
    remote(wfin.at[core], wfin.at[other], wf_s, wf_r, batch=other).wait_recv()
    gw_ref[pl.ds(pl.multiple_of(other * wrow, wrow), wrow)] = wfin[other].astype(F32)
    wf.wait_send()

    run_if(has_right, to_right.wait_send)
    run_if(has_left, to_left.wait_send)
    for b in range(cross):
        for c in sib_copies(b):
            c.wait_send()
    run_if(has_left, rim_left.wait_send)
    run_if(has_right, rim_right.wait_send)


def body(queries, key_states, value_states, grad_out, out_weight):
    n = lax.axis_size("ctx")
    rows, wide = queries.shape[1:]
    heads = wide // HD
    cross = n.bit_length() - 1
    width = grad_out.shape[2]
    coarse = sum(rows >> l for l in range(1, (rows // LEAF).bit_length() - 1 + cross))
    wrow = wide // 2
    piece = wrow // n
    pieces = n - 1
    vm = pltpu.VMEM
    dma = pltpu.SemaphoreType.DMA
    scratch = [
        vm((rows + 2 * LEAF, 2 * wide), BF16),
        vm((rows // 2, 2 * wide), BF16),
        vm((cross, LEAF, 2 * wide), BF16),
        vm((coarse, wide), BF16),
        vm((rows, wide), BF16),
        vm((cross, LEAF, 2 * wide), BF16),
        vm((rows, wide), BF16),
        vm((heads, rows, 3 * LEAF), BF16),
        vm((rows, wide), BF16),
        vm((heads, rows, HD), F32),
        vm((heads, coarse, LEAF), BF16),
        vm((heads, coarse, HD), BF16),
        vm((heads, coarse, HD), F32),
        vm((coarse, HD), F32),
        vm((coarse, HD), F32),
        vm((rows, HD), F32),
        vm((rows, HD), F32),
        vm((rows, HD), F32),
        vm((rows + 2 * LEAF, 2 * wide), F32),
        vm((rows // 2, 2 * wide), F32),
        vm((cross, LEAF, 2 * wide), BF16),
        vm((pieces, LEAF, 2 * wide), BF16),
        vm((2, LEAF, 2 * wide), BF16),
        vm((2, LEAF, 2 * wide), BF16),
        vm((coarse, wide), F32),
        vm((wide, width), F32),
        vm((wrow, width), BF16),
        vm((wrow, width), BF16),
        vm((wrow, width), BF16),
        vm((pieces, piece, width), BF16),
        vm((2, wrow, width), BF16),
        dma((2,)), dma((2,)),
        dma((pieces,)), dma((pieces,)),
        dma((pieces,)), dma((pieces,)),
        dma((2,)), dma((2,)),
        dma, dma,
        dma((pieces,)), dma((pieces,)),
        dma((pieces,)), dma((pieces,)),
        dma, dma,
    ]
    spec = pl.BlockSpec(memory_space=pltpu.VMEM)
    out = pl.pallas_call(
        functools.partial(kernel, n, heads, rows),
        out_shape=[jax.ShapeDtypeStruct((rows, wide), BF16)] * 3
        + [jax.ShapeDtypeStruct((wide, width), F32)],
        in_specs=[spec] * 5,
        out_specs=[spec] * 4,
        scratch_shapes=scratch,
        compiler_params=pltpu.CompilerParams(
            collective_id=0, has_side_effects=True, vmem_limit_bytes=56 * 2**20
        ),
    )(queries[0], key_states[0], value_states[0], grad_out[0], out_weight)
    return out[0][None], out[1][None], out[2][None], out[3]


def solution(mesh):
    row = P(("groups", "batch"), "ctx", "head")
    in_specs = (row, row, row, P(("groups", "batch"), "ctx", None), P("head", None))
    out_specs = (row, row, row, P(("groups", "head"), None))
    return jax.shard_map(body, mesh=mesh, in_specs=in_specs, out_specs=out_specs, check_vma=False)
```

```python
import functools
import math

import jax
import jax.numpy as jnp
from jax import lax
from jax.experimental import pallas as pl
from jax.experimental.pallas import tpu as pltpu
from jax.sharding import PartitionSpec as P

HD = 128
LEAF = 128
NEG_BIG = -1e30
F32 = jnp.float32
BF16 = jnp.bfloat16


def nn(a, b):
    return lax.dot_general(a, b, (((1,), (0,)), ((), ())), preferred_element_type=F32)


def nt(a, b):
    return lax.dot_general(a, b, (((1,), (1,)), ((), ())), preferred_element_type=F32)


def tn(a, b):
    return lax.dot_general(a, b, (((0,), (0,)), ((), ())), preferred_element_type=F32)


def pool_matrix(rows, entry):
    r = lax.broadcasted_iota(jnp.int32, (rows, 2 * rows), 0)
    c = lax.broadcasted_iota(jnp.int32, (rows, 2 * rows), 1)
    return jnp.where((c == 2 * r) | (c == 2 * r + 1), entry, 0.0).astype(BF16)


def spread_matrix(rows, entry):
    r = lax.broadcasted_iota(jnp.int32, (2 * rows, rows), 0)
    c = lax.broadcasted_iota(jnp.int32, (2 * rows, rows), 1)
    return jnp.where((r == 2 * c) | (r == 2 * c + 1), entry, 0.0).astype(BF16)


def kernel(
    n, heads, rows, halves,
    q_ref, k_ref, v_ref, go_ref, w_ref,
    dq_ref, dk_ref, dv_ref, wf_ref,
    kp, kv1, kvl, ql, ga, sib, attn, e0, g0, d0, el, gl, dl, fal, fbl,
    xa, xb, xc, dkp, dkv1, gout, gin, rout, rin, dql,
    wpart, wsend, wrecv, wacc, wtx, wrx, wfin,
    halo_s, halo_r, sib_s, sib_r, gs_s, gs_r, rim_s, rim_r, wp_s, wp_r, rs_s, rs_r, ag_s, ag_r, wf_s, wf_r,
):
    MESH = pl.DeviceIdType.MESH
    ctx = lax.axis_index("ctx")
    core = lax.axis_index("batch")
    other = 1 - core
    cross = n.bit_length() - 1
    wide = heads * HD
    blocks = rows // LEAF
    local = blocks.bit_length() - 1
    levels = list(range(1, local + cross))
    top = levels[-1]
    scale = HD ** (-0.5)
    c2 = scale * math.log2(math.e)

    def at(l):
        return sum(rows >> i for i in range(1, l))

    barrier = pltpu.get_barrier_semaphore()
    for m in range(1, n):
        pl.semaphore_signal(barrier, inc=1, device_id={"ctx": ctx ^ m}, device_id_type=MESH)
    pl.semaphore_signal(barrier, inc=1, device_id={"batch": other}, device_id_type=MESH)

    per = heads // halves
    hw = per * HD

    def kcol(h):
        return pl.ds(pl.multiple_of((h // per) * 2 * hw + lax.rem(h, per) * HD, HD), HD)

    def vcol(h):
        return pl.ds(pl.multiple_of((h // per) * 2 * hw + hw + lax.rem(h, per) * HD, HD), HD)

    def hcol(u):
        return pl.ds(u * 2 * hw, 2 * hw)

    for u in range(halves):
        kp[LEAF : LEAF + rows, u * 2 * hw : u * 2 * hw + hw] = k_ref[:, u * hw : (u + 1) * hw]
        kp[LEAF : LEAF + rows, u * 2 * hw + hw : (u + 1) * 2 * hw] = v_ref[:, u * hw : (u + 1) * hw]

    half = pool_matrix(LEAF, 0.5)

    def pool(x, cnt):
        return nn(half[: cnt, : 2 * cnt], x).astype(BF16)

    for b in range(blocks // 2):
        kv1[b * LEAF : (b + 1) * LEAF] = pool(kp[LEAF + 2 * b * LEAF : LEAF + 2 * (b + 1) * LEAF], LEAF)
    kv2 = pool(kv1[...], LEAF)
    for b in range(cross):
        cnt = LEAF >> b
        kvl[b, :cnt] = kv2
        if b + 1 < cross:
            kv2 = pool(kv2, cnt // 2)

    @pl.when(ctx == 0)
    def _():
        kp[:LEAF] = jnp.zeros((LEAF, 2 * wide), BF16)

    @pl.when(ctx == n - 1)
    def _():
        kp[LEAF + rows :] = jnp.zeros((LEAF, 2 * wide), BF16)

    pl.semaphore_wait(barrier, n)

    def remote(src, dst, s, r, **dev):
        return pltpu.make_async_remote_copy(
            src_ref=src, dst_ref=dst, send_sem=s, recv_sem=r, device_id=dev, device_id_type=MESH
        )

    right = jnp.minimum(ctx + 1, n - 1)
    left = jnp.maximum(ctx - 1, 0)

    def to_right(u):
        return remote(kp.at[pl.ds(rows, LEAF), hcol(u)], kp.at[pl.ds(0, LEAF), hcol(u)],
                      halo_s.at[u, 0], halo_r.at[u, 0], ctx=right)

    def to_left(u):
        return remote(kp.at[pl.ds(LEAF, LEAF), hcol(u)], kp.at[pl.ds(rows + LEAF, LEAF), hcol(u)],
                      halo_s.at[u, 1], halo_r.at[u, 1], ctx=left)

    has_right = ctx < n - 1
    has_left = ctx > 0

    def run_if(cond, fn):
        @pl.when(cond)
        def _():
            fn()

    def sib_copies(u, b):
        cnt = LEAF >> b
        mine = lax.rem(ctx, 1 << b) * cnt
        out = []
        for j in range(1 << b):
            peer = ctx ^ ((1 << b) | j)
            slot = (1 << b) - 1 + j
            out.append(remote(
                kvl.at[b, pl.ds(0, cnt), hcol(u)], sib.at[b, pl.ds(pl.multiple_of(mine, cnt), cnt), hcol(u)],
                sib_s.at[u, slot], sib_r.at[u, slot], ctx=peer))
        return out

    def sib_arrivals(u, b):
        cnt = LEAF >> b
        out = []
        for j in range(1 << b):
            peer = ctx ^ ((1 << b) | j)
            slot = (1 << b) - 1 + j
            theirs = lax.rem(peer, 1 << b) * cnt
            out.append(remote(
                kvl.at[b, pl.ds(0, cnt), hcol(u)], sib.at[b, pl.ds(pl.multiple_of(theirs, cnt), cnt), hcol(u)],
                sib_s.at[u, slot], sib_r.at[u, slot], ctx=peer))
        return out

    def send_kv(u):
        run_if(has_right, to_right(u).start)
        run_if(has_left, to_left(u).start)
        for b in range(cross):
            for c in sib_copies(u, b):
                c.start()

    def take_kv(u):
        run_if(has_left, to_right(u).wait_recv)
        run_if(has_right, to_left(u).wait_recv)
        for b in range(cross):
            for c in sib_arrivals(u, b):
                c.wait_recv()

    def sent_kv(u):
        run_if(has_right, to_right(u).wait_send)
        run_if(has_left, to_left(u).wait_send)
        for b in range(cross):
            for c in sib_copies(u, b):
                c.wait_send()

    send_kv(0)

    for b in range(blocks // 2):
        ql[b * LEAF : (b + 1) * LEAF] = pool(q_ref[2 * b * LEAF : 2 * (b + 1) * LEAF], LEAF)
    for l in levels[1:]:
        cnt = rows >> l
        ql[at(l) : at(l) + cnt] = pool(ql[at(l - 1) : at(l - 1) + 2 * cnt], cnt)
    for b in range(blocks):
        ga[b * LEAF : (b + 1) * LEAF] = nt(go_ref[b * LEAF : (b + 1) * LEAF], w_ref[...]).astype(BF16)

    def coarse_keys(l):
        if l < local:
            return [
                (c * LEAF, LEAF, kv1, (c ^ 1) * LEAF) for c in range((rows >> l) // LEAF)
            ]
        return [(0, rows >> l, sib.at[l - local], 0)]

    def wide_row(x, cnt):
        return jnp.broadcast_to(x, (cnt, HD))

    def spread(ref, x, cnt):
        ref[pl.ds(0, cnt, stride=2), :] = x
        ref[pl.ds(1, cnt, stride=2), :] = x
        return ref[pl.ds(0, 2 * cnt), :]

    def gather_pairs(ref, x, cnt):
        ref[pl.ds(0, 2 * cnt), :] = x
        return ref[pl.ds(0, cnt, stride=2), :] + ref[pl.ds(1, cnt, stride=2), :]

    def forward(h, carry):
        hs = pl.ds(pl.multiple_of(h * HD, HD), HD)
        ks = kcol(h)
        vs = vcol(h)
        acc = None
        for l in reversed(levels):
            parts = []
            for r0, cnt, ref, k0 in coarse_keys(l):
                s = nt(ql[at(l) + r0 : at(l) + r0 + cnt, hs], ref[k0 : k0 + LEAF, ks]) * c2
                m = wide_row(jnp.max(s, axis=1, keepdims=True), cnt)
                e = jnp.exp2(s - m)
                eb = e.astype(BF16)
                el[h, at(l) + r0 : at(l) + r0 + cnt] = eb
                parts.append((m, wide_row(jnp.sum(e, axis=1, keepdims=True), cnt), nn(eb, ref[k0 : k0 + LEAF, vs])))
            m, s, o = [jnp.concatenate(x) if len(x) > 1 else x[0] for x in zip(*parts)]
            cnt = rows >> l
            if acc is None:
                acc = (m, s, o)
                fal[at(l) : at(l) + cnt] = jnp.ones((cnt, HD), F32)
            else:
                am, as_, ao = [spread(r, x, cnt // 2) for r, x in zip((xa, xb, xc), acc)]
                nm = jnp.maximum(m, am)
                fa = jnp.exp2(m - nm)
                fb = jnp.exp2(am - nm)
                fal[at(l) : at(l) + cnt] = fa
                fbl[at(l) : at(l) + cnt] = fb
                acc = (nm, fa * s + fb * as_, fa * o + fb * ao)
        am, as_, ao = [spread(r, x, rows // 2) for r, x in zip((xa, xb, xc), acc)]
        mixed = []
        for b in range(blocks):
            br = slice(b * LEAF, (b + 1) * LEAF)
            kr = slice(b * LEAF, (b + 3) * LEAF)
            s = nt(q_ref[br, hs], kp[kr, ks]) * c2
            if b == 0:
                col = lax.broadcasted_iota(jnp.int32, s.shape, 1)
                s = jnp.where((col >= LEAF) | has_left, s, NEG_BIG)
            if b == blocks - 1:
                col = lax.broadcasted_iota(jnp.int32, s.shape, 1)
                s = jnp.where((col < 2 * LEAF) | has_right, s, NEG_BIG)
            m = wide_row(jnp.max(s, axis=1, keepdims=True), LEAF)
            e = jnp.exp2(s - jnp.concatenate([m, m, m], axis=1))
            eb = e.astype(BF16)
            e0[h, br] = eb
            su = wide_row(jnp.sum(e, axis=1, keepdims=True), LEAF)
            o = nn(eb, kp[kr, vs])
            nm = jnp.maximum(m, am[br])
            fa = jnp.exp2(m - nm)
            fb = jnp.exp2(am[br] - nm)
            inv = 1.0 / (fa * su + fb * as_[br])
            at_b = ((fa * o + fb * ao[br]) * inv).astype(BF16)
            attn[br, hs] = at_b
            af = at_b.astype(F32)
            g = ga[br, hs].astype(F32)
            gb = (g * (fa * inv)).astype(BF16)
            g0[br, hs] = gb
            d0[h, br] = wide_row(jnp.sum(gb.astype(F32) * af, axis=1, keepdims=True), LEAF)
            r1 = fb * inv
            mixed.append((g * r1, r1 * wide_row(jnp.sum(g * af, axis=1, keepdims=True), LEAF)))
        gc = jnp.concatenate([x[0] for x in mixed])
        dc = jnp.concatenate([x[1] for x in mixed])
        for l in levels:
            cnt = rows >> l
            gc = gather_pairs(xa, gc, cnt)
            dc = gather_pairs(xb, dc, cnt)
            fa = fal[at(l) : at(l) + cnt]
            gl[h, at(l) : at(l) + cnt] = (gc * fa).astype(BF16)
            dl[h, at(l) : at(l) + cnt] = dc * fa
            if l != top:
                fb = fbl[at(l) : at(l) + cnt]
                gc = gc * fb
                dc = dc * fb
        return carry

    half_cols = go_ref.shape[1] // 2
    steps = cross
    my_cols = pl.ds(pl.multiple_of(core * half_cols, half_cols), half_cols)
    other_cols = pl.ds(pl.multiple_of(other * half_cols, half_cols), half_cols)

    def bit(s):
        return lax.rem(ctx // (1 << s), 2)

    def weight_grad(u):
        for b in range(per):
            wpart[u, b * HD : (b + 1) * HD] = tn(attn[:, u * hw + b * HD : u * hw + (b + 1) * HD], go_ref[...])
        wsend[u] = wpart[u, :, other_cols].astype(BF16)
        pair = remote(wsend.at[u], wrecv.at[u], wp_s.at[u], wp_r.at[u], batch=other)
        pair.start()
        yield
        pair.wait()
        wacc[u] = wpart[u, :, my_cols] + wrecv[u].astype(F32)
        lo, size, got = 0, hw, 0
        for s in range(steps):
            size //= 2
            give = pl.multiple_of(lo + (1 - bit(s)) * size, size)
            lo = lo + bit(s) * size
            keep = pl.multiple_of(lo, size)
            wtx[u, pl.ds(give, size)] = wacc[u, pl.ds(give, size)].astype(BF16)
            c = remote(wtx.at[u, pl.ds(give, size)], wrx.at[u, pl.ds(got, size)],
                       rs_s.at[u, s], rs_r.at[u, s], ctx=ctx ^ (1 << s))
            c.start()
            yield
            c.wait()
            wacc[u, pl.ds(keep, size)] += wrx[u, pl.ds(got, size)].astype(F32)
            got += size
        wfin[u, core, pl.ds(pl.multiple_of(lo, size), size)] = wacc[u, pl.ds(pl.multiple_of(lo, size), size)].astype(BF16)
        for s in reversed(range(steps)):
            mine = pl.ds(pl.multiple_of(lo, size), size)
            theirs = pl.ds(pl.multiple_of(lo + (1 - 2 * bit(s)) * size, size), size)
            peer = ctx ^ (1 << s)
            c = remote(wfin.at[u, core, mine], wfin.at[u, core, mine], ag_s.at[u, s], ag_r.at[u, s], ctx=peer)
            c.start()
            yield
            c.wait_send()
            remote(wfin.at[u, core, mine], wfin.at[u, core, theirs], ag_s.at[u, s], ag_r.at[u, s], ctx=peer).wait_recv()
            lo = lo - bit(s) * size
            size *= 2
        c = remote(wfin.at[u, core], wfin.at[u, core], wf_s.at[u], wf_r.at[u], batch=other)
        c.start()
        yield
        c.wait_send()
        remote(wfin.at[u, core], wfin.at[u, other], wf_s.at[u], wf_r.at[u], batch=other).wait_recv()

    def coarse_back(h, l):
        hs = pl.ds(pl.multiple_of(h * HD, HD), HD)
        ks = kcol(h)
        vs = vcol(h)
        for r0, cnt, ref, k0 in coarse_keys(l):
            r = slice(at(l) + r0, at(l) + r0 + cnt)
            keys = ref[k0 : k0 + LEAF, ks]
            eb = el[h, r]
            g = gl[h, r]
            inner = nt(g, ref[k0 : k0 + LEAF, vs])
            ds = (eb.astype(F32) * (inner - dl[h, r])).astype(BF16)
            dql[r, hs] = nn(ds, keys) * scale
            dk = tn(ds, ql[r, hs]) * scale
            dv = tn(eb, g)
            if l < local:
                dkv1[k0 : k0 + LEAF, ks] = dk
                dkv1[k0 : k0 + LEAF, vs] = dv
            else:
                gout[l - local, :, ks] = dk.astype(BF16)
                gout[l - local, :, vs] = dv.astype(BF16)

    def back_cross(h, carry):
        for l in levels[local - 1 :]:
            coarse_back(h, l)
        return carry

    def grad_copies(u, b):
        cnt = LEAF >> b
        out = []
        for j in range(1 << b):
            peer = ctx ^ ((1 << b) | j)
            slot = (1 << b) - 1 + j
            theirs = lax.rem(peer, 1 << b) * cnt
            out.append(remote(
                gout.at[b, pl.ds(pl.multiple_of(theirs, cnt), cnt), hcol(u)], gin.at[slot, pl.ds(0, cnt), hcol(u)],
                gs_s.at[u, slot], gs_r.at[u, slot], ctx=peer))
        return out

    dkp[...] = jnp.zeros_like(dkp)

    def back_level0(h, carry):
        hs = pl.ds(pl.multiple_of(h * HD, HD), HD)
        ks = kcol(h)
        vs = vcol(h)
        for b in range(blocks):
            br = slice(b * LEAF, (b + 1) * LEAF)
            kr = slice(b * LEAF, (b + 3) * LEAF)
            eb = e0[h, br]
            gb = g0[br, hs]
            keys = kp[kr, ks]
            d = d0[h, br]
            inner = nt(gb, kp[kr, vs])
            ds = (eb.astype(F32) * (inner - jnp.concatenate([d, d, d], axis=1))).astype(BF16)
            xc[br] = nn(ds, keys) * scale
            dkp[kr, ks] += tn(ds, q_ref[br, hs]) * scale
            dkp[kr, vs] += tn(eb, gb)
        for l in levels[: local - 1]:
            coarse_back(h, l)
        chain = None
        for l in reversed(levels):
            cnt = rows >> l
            x = dql[at(l) : at(l) + cnt, hs]
            if chain is not None:
                x = x + spread(xa, chain * 0.5, cnt // 2)
            chain = x
        dq_ref[:, hs] = (xc[...] + spread(xa, chain * 0.5, rows // 2)).astype(BF16)
        return carry

    def rim_left(u):
        return remote(rout.at[0, :, hcol(u)], rin.at[1, :, hcol(u)], rim_s.at[u, 0], rim_r.at[u, 1], ctx=left)

    def rim_right(u):
        return remote(rout.at[1, :, hcol(u)], rin.at[0, :, hcol(u)], rim_s.at[u, 1], rim_r.at[u, 0], ctx=right)

    twice = spread_matrix(LEAF, 0.5)

    def spread_wide(x, cnt):
        return nn(twice[: 2 * cnt, : cnt], x.astype(BF16))

    def send_grads(u):
        for b in range(cross):
            for c in grad_copies(u, b):
                c.start()

    def send_rims(u):
        rout[0, :, hcol(u)] = dkp[:LEAF, hcol(u)].astype(BF16)
        rout[1, :, hcol(u)] = dkp[LEAF + rows :, hcol(u)].astype(BF16)
        run_if(has_left, rim_left(u).start)
        run_if(has_right, rim_right(u).start)

    def finish(u):
        for b in range(cross):
            for c in grad_copies(u, b):
                c.wait()
        chain = None
        for b in reversed(range(cross)):
            cnt = LEAF >> b
            x = 0.0
            for j in range(1 << b):
                x = x + gin[(1 << b) - 1 + j, :cnt, hcol(u)].astype(F32)
            if chain is not None:
                x = x + spread_wide(chain, cnt // 2)
            chain = x
        dkv1[:, hcol(u)] += spread_wide(chain, LEAF)
        for b in range(blocks // 2):
            dkp[LEAF * (1 + 2 * b) : LEAF * (3 + 2 * b), hcol(u)] += spread_wide(
                dkv1[b * LEAF : (b + 1) * LEAF, hcol(u)], LEAF)

        def left_arrival():
            rim_right(u).wait_recv()
            dkp[LEAF : 2 * LEAF, hcol(u)] += rin[0, :, hcol(u)].astype(F32)

        def right_arrival():
            rim_left(u).wait_recv()
            dkp[rows : rows + LEAF, hcol(u)] += rin[1, :, hcol(u)].astype(F32)

        run_if(has_left, left_arrival)
        run_if(has_right, right_arrival)
        dk_ref[:, u * hw : (u + 1) * hw] = dkp[LEAF : LEAF + rows, u * 2 * hw : u * 2 * hw + hw].astype(BF16)
        dv_ref[:, u * hw : (u + 1) * hw] = dkp[LEAF : LEAF + rows, u * 2 * hw + hw : (u + 1) * 2 * hw].astype(BF16)

    chains = []

    def advance():
        for c in list(chains):
            if next(c, chains) is chains:
                chains.remove(c)

    for u in range(halves):
        take_kv(u)
        if u + 1 < halves:
            send_kv(u + 1)
        lax.fori_loop(u * per, (u + 1) * per, forward, 0)
        chains.append(weight_grad(u))
        advance()
        lax.fori_loop(u * per, (u + 1) * per, back_cross, 0)
        send_grads(u)
        advance()
        lax.fori_loop(u * per, (u + 1) * per, back_level0, 0)
        send_rims(u)
        advance()
    for u in range(halves):
        finish(u)
        advance()
    while chains:
        advance()
    wf_ref[...] = wfin[...]
    for u in range(halves):
        sent_kv(u)
        run_if(has_left, rim_left(u).wait_send)
        run_if(has_right, rim_right(u).wait_send)


def settle(dq_in, dk_in, dv_in, wf, dq, dk, dv, gw):
    dq[...] = dq_in[...]
    dk[...] = dk_in[...]
    dv[...] = dv_in[...]
    halves, cores, size, cols = wf.shape
    for u in range(halves):
        for c in range(cores):
            gw[u * size : (u + 1) * size, c * cols : (c + 1) * cols] = wf[u, c].astype(F32)


def body(queries, key_states, value_states, grad_out, out_weight):
    n = lax.axis_size("ctx")
    rows, wide = queries.shape[1:]
    heads = wide // HD
    cross = n.bit_length() - 1
    width = grad_out.shape[2]
    coarse = sum(rows >> l for l in range(1, (rows // LEAF).bit_length() - 1 + cross))
    halves = 2 if heads % 2 == 0 and wide // 2 // n >= 16 else 1
    hw = wide // halves
    cols = width // 2
    pieces = n - 1
    vm = pltpu.VMEM
    dma = pltpu.SemaphoreType.DMA
    scratch = [
        vm((rows + 2 * LEAF, 2 * wide), BF16),
        vm((rows // 2, 2 * wide), BF16),
        vm((cross, LEAF, 2 * wide), BF16),
        vm((coarse, wide), BF16),
        vm((rows, wide), BF16),
        vm((cross, LEAF, 2 * wide), BF16),
        vm((rows, wide), BF16),
        vm((heads, rows, 3 * LEAF), BF16),
        vm((rows, wide), BF16),
        vm((heads, rows, HD), F32),
        vm((heads, coarse, LEAF), BF16),
        vm((heads, coarse, HD), BF16),
        vm((heads, coarse, HD), F32),
        vm((coarse, HD), F32),
        vm((coarse, HD), F32),
        vm((rows, HD), F32),
        vm((rows, HD), F32),
        vm((rows, HD), F32),
        vm((rows + 2 * LEAF, 2 * wide), F32),
        vm((rows // 2, 2 * wide), F32),
        vm((cross, LEAF, 2 * wide), BF16),
        vm((pieces, LEAF, 2 * wide), BF16),
        vm((2, LEAF, 2 * wide), BF16),
        vm((2, LEAF, 2 * wide), BF16),
        vm((coarse, wide), F32),
        vm((halves, hw, width), F32),
        vm((halves, hw, cols), BF16),
        vm((halves, hw, cols), BF16),
        vm((halves, hw, cols), F32),
        vm((halves, hw, cols), BF16),
        vm((halves, hw, cols), BF16),
        vm((halves, 2, hw, cols), BF16),
        dma((halves, 2)), dma((halves, 2)),
        dma((halves, pieces)), dma((halves, pieces)),
        dma((halves, pieces)), dma((halves, pieces)),
        dma((halves, 2)), dma((halves, 2)),
        dma((halves,)), dma((halves,)),
        dma((halves, cross)), dma((halves, cross)),
        dma((halves, cross)), dma((halves, cross)),
        dma((halves,)), dma((halves,)),
    ]
    spec = pl.BlockSpec(memory_space=pltpu.VMEM)
    out = pl.pallas_call(
        functools.partial(kernel, n, heads, rows, halves),
        out_shape=[jax.ShapeDtypeStruct((rows, wide), BF16)] * 3
        + [jax.ShapeDtypeStruct((halves, 2, hw, cols), BF16)],
        in_specs=[spec] * 5,
        out_specs=[spec] * 4,
        scratch_shapes=scratch,
        compiler_params=pltpu.CompilerParams(
            collective_id=0, has_side_effects=True, vmem_limit_bytes=56 * 2**20
        ),
    )(queries[0], key_states[0], value_states[0], grad_out[0], out_weight)
    small = jax.ShapeDtypeStruct((rows, wide), BF16)
    dq, dk, dv, gw = pl.pallas_call(
        settle,
        out_shape=[small, small, small, jax.ShapeDtypeStruct((wide, width), F32)],
        in_specs=[spec] * 4,
        out_specs=[spec] * 4,
    )(*out)
    return dq[None], dk[None], dv[None], gw


def solution(mesh):
    row = P(("groups", "batch"), "ctx", "head")
    in_specs = (row, row, row, P(("groups", "batch"), "ctx", None), P("head", None))
    out_specs = (row, row, row, P(("groups", "head"), None))
    return jax.shard_map(body, mesh=mesh, in_specs=in_specs, out_specs=out_specs, check_vma=False)
```

```python
import functools
import math

import jax
import jax.numpy as jnp
from jax import lax
from jax.experimental import pallas as pl
from jax.experimental.pallas import tpu as pltpu
from jax.sharding import PartitionSpec as P

HD = 128
LEAF = 128
NEG_BIG = -1e30
F32 = jnp.float32
BF16 = jnp.bfloat16


def nn(a, b):
    return lax.dot_general(a, b, (((1,), (0,)), ((), ())), preferred_element_type=F32)


def nt(a, b):
    return lax.dot_general(a, b, (((1,), (1,)), ((), ())), preferred_element_type=F32)


def tn(a, b):
    return lax.dot_general(a, b, (((0,), (0,)), ((), ())), preferred_element_type=F32)


def pool_matrix(rows, entry):
    r = lax.broadcasted_iota(jnp.int32, (rows, 2 * rows), 0)
    c = lax.broadcasted_iota(jnp.int32, (rows, 2 * rows), 1)
    return jnp.where((c == 2 * r) | (c == 2 * r + 1), entry, 0.0).astype(BF16)


def spread_matrix(rows, entry):
    r = lax.broadcasted_iota(jnp.int32, (2 * rows, rows), 0)
    c = lax.broadcasted_iota(jnp.int32, (2 * rows, rows), 1)
    return jnp.where((r == 2 * c) | (r == 2 * c + 1), entry, 0.0).astype(BF16)


def kernel(
    n, heads, rows, halves,
    q_ref, k_ref, v_ref, go_ref, w_ref,
    dq_ref, dk_ref, dv_ref, wf_ref,
    kp, kv1, kvl, ql, ga, sib, attn, e0, g0, d0, el, gl, dl, fal, fbl,
    xa, xb, xc, dkp, dkv1, gout, gin, rout, rin, dql,
    wpart, wsend, wrecv, wacc, wtx, wrx, wfin,
    halo_s, halo_r, sib_s, sib_r, gs_s, gs_r, rim_s, rim_r, wp_s, wp_r, rs_s, rs_r, ag_s, ag_r, wf_s, wf_r,
):
    MESH = pl.DeviceIdType.MESH
    ctx = lax.axis_index("ctx")
    core = lax.axis_index("batch")
    other = 1 - core
    cross = n.bit_length() - 1
    wide = heads * HD
    blocks = rows // LEAF
    local = blocks.bit_length() - 1
    levels = list(range(1, local + cross))
    top = levels[-1]
    scale = HD ** (-0.5)
    c2 = scale * math.log2(math.e)

    def at(l):
        return sum(rows >> i for i in range(1, l))

    barrier = pltpu.get_barrier_semaphore()
    for m in range(1, n):
        pl.semaphore_signal(barrier, inc=1, device_id={"ctx": ctx ^ m}, device_id_type=MESH)
    pl.semaphore_signal(barrier, inc=1, device_id={"batch": other}, device_id_type=MESH)

    per = heads // halves
    hw = per * HD

    def kcol(h):
        return pl.ds(pl.multiple_of((h // per) * 2 * hw + lax.rem(h, per) * HD, HD), HD)

    def vcol(h):
        return pl.ds(pl.multiple_of((h // per) * 2 * hw + hw + lax.rem(h, per) * HD, HD), HD)

    def hcol(u):
        return pl.ds(u * 2 * hw, 2 * hw)

    for u in range(halves):
        kp[LEAF : LEAF + rows, u * 2 * hw : u * 2 * hw + hw] = k_ref[:, u * hw : (u + 1) * hw]
        kp[LEAF : LEAF + rows, u * 2 * hw + hw : (u + 1) * 2 * hw] = v_ref[:, u * hw : (u + 1) * hw]

    half = pool_matrix(LEAF, 0.5)

    def pool(x, cnt):
        return nn(half[: cnt, : 2 * cnt], x).astype(BF16)

    for b in range(blocks // 2):
        kv1[b * LEAF : (b + 1) * LEAF] = pool(kp[LEAF + 2 * b * LEAF : LEAF + 2 * (b + 1) * LEAF], LEAF)
    kv2 = pool(kv1[...], LEAF)
    for b in range(cross):
        cnt = LEAF >> b
        kvl[b, :cnt] = kv2
        if b + 1 < cross:
            kv2 = pool(kv2, cnt // 2)

    @pl.when(ctx == 0)
    def _():
        kp[:LEAF] = jnp.zeros((LEAF, 2 * wide), BF16)

    @pl.when(ctx == n - 1)
    def _():
        kp[LEAF + rows :] = jnp.zeros((LEAF, 2 * wide), BF16)

    pl.semaphore_wait(barrier, n)

    def remote(src, dst, s, r, **dev):
        return pltpu.make_async_remote_copy(
            src_ref=src, dst_ref=dst, send_sem=s, recv_sem=r, device_id=dev, device_id_type=MESH
        )

    right = jnp.minimum(ctx + 1, n - 1)
    left = jnp.maximum(ctx - 1, 0)

    def to_right(u):
        return remote(kp.at[pl.ds(rows, LEAF), hcol(u)], kp.at[pl.ds(0, LEAF), hcol(u)],
                      halo_s.at[u, 0], halo_r.at[u, 0], ctx=right)

    def to_left(u):
        return remote(kp.at[pl.ds(LEAF, LEAF), hcol(u)], kp.at[pl.ds(rows + LEAF, LEAF), hcol(u)],
                      halo_s.at[u, 1], halo_r.at[u, 1], ctx=left)

    has_right = ctx < n - 1
    has_left = ctx > 0

    def run_if(cond, fn):
        @pl.when(cond)
        def _():
            fn()

    def sib_copies(u, b):
        cnt = LEAF >> b
        mine = lax.rem(ctx, 1 << b) * cnt
        out = []
        for j in range(1 << b):
            peer = ctx ^ ((1 << b) | j)
            slot = (1 << b) - 1 + j
            out.append(remote(
                kvl.at[b, pl.ds(0, cnt), hcol(u)], sib.at[b, pl.ds(pl.multiple_of(mine, cnt), cnt), hcol(u)],
                sib_s.at[u, slot], sib_r.at[u, slot], ctx=peer))
        return out

    def sib_arrivals(u, b):
        cnt = LEAF >> b
        out = []
        for j in range(1 << b):
            peer = ctx ^ ((1 << b) | j)
            slot = (1 << b) - 1 + j
            theirs = lax.rem(peer, 1 << b) * cnt
            out.append(remote(
                kvl.at[b, pl.ds(0, cnt), hcol(u)], sib.at[b, pl.ds(pl.multiple_of(theirs, cnt), cnt), hcol(u)],
                sib_s.at[u, slot], sib_r.at[u, slot], ctx=peer))
        return out

    def send_kv(u):
        run_if(has_right, to_right(u).start)
        run_if(has_left, to_left(u).start)
        for b in range(cross):
            for c in sib_copies(u, b):
                c.start()

    def take_kv(u):
        run_if(has_left, to_right(u).wait_recv)
        run_if(has_right, to_left(u).wait_recv)
        for b in range(cross):
            for c in sib_arrivals(u, b):
                c.wait_recv()

    def sent_kv(u):
        run_if(has_right, to_right(u).wait_send)
        run_if(has_left, to_left(u).wait_send)
        for b in range(cross):
            for c in sib_copies(u, b):
                c.wait_send()

    for u in range(halves):
        send_kv(u)

    for b in range(blocks // 2):
        ql[b * LEAF : (b + 1) * LEAF] = pool(q_ref[2 * b * LEAF : 2 * (b + 1) * LEAF], LEAF)
    for l in levels[1:]:
        cnt = rows >> l
        ql[at(l) : at(l) + cnt] = pool(ql[at(l - 1) : at(l - 1) + 2 * cnt], cnt)
    for b in range(blocks):
        ga[b * LEAF : (b + 1) * LEAF] = nt(go_ref[b * LEAF : (b + 1) * LEAF], w_ref[...]).astype(BF16)

    def coarse_keys(l):
        if l < local:
            return [
                (c * LEAF, LEAF, kv1, (c ^ 1) * LEAF) for c in range((rows >> l) // LEAF)
            ]
        return [(0, rows >> l, sib.at[l - local], 0)]

    def wide_row(x, cnt):
        return jnp.broadcast_to(x, (cnt, HD))

    def spread(ref, x, cnt):
        ref[pl.ds(0, cnt, stride=2), :] = x
        ref[pl.ds(1, cnt, stride=2), :] = x
        return ref[pl.ds(0, 2 * cnt), :]

    def gather_pairs(ref, x, cnt):
        ref[pl.ds(0, 2 * cnt), :] = x
        return ref[pl.ds(0, cnt, stride=2), :] + ref[pl.ds(1, cnt, stride=2), :]

    def forward(h, carry):
        hs = pl.ds(pl.multiple_of(h * HD, HD), HD)
        ks = kcol(h)
        vs = vcol(h)
        acc = None
        for l in reversed(levels):
            parts = []
            for r0, cnt, ref, k0 in coarse_keys(l):
                s = nt(ql[at(l) + r0 : at(l) + r0 + cnt, hs], ref[k0 : k0 + LEAF, ks]) * c2
                m = wide_row(jnp.max(s, axis=1, keepdims=True), cnt)
                e = jnp.exp2(s - m)
                eb = e.astype(BF16)
                el[h, at(l) + r0 : at(l) + r0 + cnt] = eb
                parts.append((m, wide_row(jnp.sum(e, axis=1, keepdims=True), cnt), nn(eb, ref[k0 : k0 + LEAF, vs])))
            m, s, o = [jnp.concatenate(x) if len(x) > 1 else x[0] for x in zip(*parts)]
            cnt = rows >> l
            if acc is None:
                acc = (m, s, o)
                fal[at(l) : at(l) + cnt] = jnp.ones((cnt, HD), F32)
            else:
                am, as_, ao = [spread(r, x, cnt // 2) for r, x in zip((xa, xb, xc), acc)]
                nm = jnp.maximum(m, am)
                fa = jnp.exp2(m - nm)
                fb = jnp.exp2(am - nm)
                fal[at(l) : at(l) + cnt] = fa
                fbl[at(l) : at(l) + cnt] = fb
                acc = (nm, fa * s + fb * as_, fa * o + fb * ao)
        am, as_, ao = [spread(r, x, rows // 2) for r, x in zip((xa, xb, xc), acc)]
        mixed = []
        for b in range(blocks):
            br = slice(b * LEAF, (b + 1) * LEAF)
            kr = slice(b * LEAF, (b + 3) * LEAF)
            s = nt(q_ref[br, hs], kp[kr, ks]) * c2
            if b == 0:
                col = lax.broadcasted_iota(jnp.int32, s.shape, 1)
                s = jnp.where((col >= LEAF) | has_left, s, NEG_BIG)
            if b == blocks - 1:
                col = lax.broadcasted_iota(jnp.int32, s.shape, 1)
                s = jnp.where((col < 2 * LEAF) | has_right, s, NEG_BIG)
            m = wide_row(jnp.max(s, axis=1, keepdims=True), LEAF)
            e = jnp.exp2(s - jnp.concatenate([m, m, m], axis=1))
            eb = e.astype(BF16)
            e0[h, br] = eb
            su = wide_row(jnp.sum(e, axis=1, keepdims=True), LEAF)
            o = nn(eb, kp[kr, vs])
            nm = jnp.maximum(m, am[br])
            fa = jnp.exp2(m - nm)
            fb = jnp.exp2(am[br] - nm)
            inv = 1.0 / (fa * su + fb * as_[br])
            at_b = ((fa * o + fb * ao[br]) * inv).astype(BF16)
            attn[br, hs] = at_b
            af = at_b.astype(F32)
            g = ga[br, hs].astype(F32)
            gb = (g * (fa * inv)).astype(BF16)
            g0[br, hs] = gb
            d0[h, br] = wide_row(jnp.sum(gb.astype(F32) * af, axis=1, keepdims=True), LEAF)
            r1 = fb * inv
            mixed.append((g * r1, r1 * wide_row(jnp.sum(g * af, axis=1, keepdims=True), LEAF)))
        gc = jnp.concatenate([x[0] for x in mixed])
        dc = jnp.concatenate([x[1] for x in mixed])
        for l in levels:
            cnt = rows >> l
            gc = gather_pairs(xa, gc, cnt)
            dc = gather_pairs(xb, dc, cnt)
            fa = fal[at(l) : at(l) + cnt]
            gl[h, at(l) : at(l) + cnt] = (gc * fa).astype(BF16)
            dl[h, at(l) : at(l) + cnt] = dc * fa
            if l != top:
                fb = fbl[at(l) : at(l) + cnt]
                gc = gc * fb
                dc = dc * fb
        return carry

    half_cols = go_ref.shape[1] // 2
    my_cols = pl.ds(pl.multiple_of(core * half_cols, half_cols), half_cols)
    other_cols = pl.ds(pl.multiple_of(other * half_cols, half_cols), half_cols)

    def weight_grad(u):
        for b in range(per):
            wpart[u, b * HD : (b + 1) * HD] = tn(attn[:, u * hw + b * HD : u * hw + (b + 1) * HD], go_ref[...])
        wsend[u] = wpart[u, :, other_cols].astype(BF16)
        pair = remote(wsend.at[u], wrecv.at[u], wp_s.at[u], wp_r.at[u], batch=other)
        pair.start()
        yield
        pair.wait()
        wacc[u] = wpart[u, :, my_cols] + wrecv[u].astype(F32)
        piece = hw // n
        wtx[u] = wacc[u].astype(BF16)
        mine = pl.ds(pl.multiple_of(ctx * piece, piece), piece)

        def part(m):
            return pl.ds(pl.multiple_of((ctx ^ m) * piece, piece), piece)

        out = []
        for m in range(1, n):
            c = remote(wtx.at[u, part(m)], wrx.at[u, pl.ds((m - 1) * piece, piece)],
                       rs_s.at[u, m - 1], rs_r.at[u, m - 1], ctx=ctx ^ m)
            c.start()
            out.append(c)
        yield
        tot = wacc[u, mine]
        for m in range(1, n):
            out[m - 1].wait()
            tot = tot + wrx[u, (m - 1) * piece : m * piece].astype(F32)
        wfin[u, core, mine] = tot.astype(BF16)
        out = []
        for m in range(1, n):
            c = remote(wfin.at[u, core, mine], wfin.at[u, core, mine], ag_s.at[u, m - 1], ag_r.at[u, m - 1], ctx=ctx ^ m)
            c.start()
            out.append(c)
        yield
        for m in range(1, n):
            out[m - 1].wait_send()
            remote(wfin.at[u, core, mine], wfin.at[u, core, part(m)], ag_s.at[u, m - 1], ag_r.at[u, m - 1],
                   ctx=ctx ^ m).wait_recv()
        c = remote(wfin.at[u, core], wfin.at[u, core], wf_s.at[u], wf_r.at[u], batch=other)
        c.start()
        yield
        c.wait_send()
        remote(wfin.at[u, core], wfin.at[u, other], wf_s.at[u], wf_r.at[u], batch=other).wait_recv()

    def coarse_back(h, l):
        hs = pl.ds(pl.multiple_of(h * HD, HD), HD)
        ks = kcol(h)
        vs = vcol(h)
        for r0, cnt, ref, k0 in coarse_keys(l):
            r = slice(at(l) + r0, at(l) + r0 + cnt)
            keys = ref[k0 : k0 + LEAF, ks]
            eb = el[h, r]
            g = gl[h, r]
            inner = nt(g, ref[k0 : k0 + LEAF, vs])
            ds = (eb.astype(F32) * (inner - dl[h, r])).astype(BF16)
            dql[r, hs] = nn(ds, keys) * scale
            dk = tn(ds, ql[r, hs]) * scale
            dv = tn(eb, g)
            if l < local:
                dkv1[k0 : k0 + LEAF, ks] = dk
                dkv1[k0 : k0 + LEAF, vs] = dv
            else:
                gout[l - local, :, ks] = dk.astype(BF16)
                gout[l - local, :, vs] = dv.astype(BF16)

    def back_cross(h, carry):
        for l in levels[local - 1 :]:
            coarse_back(h, l)
        return carry

    def grad_copies(u, b):
        cnt = LEAF >> b
        out = []
        for j in range(1 << b):
            peer = ctx ^ ((1 << b) | j)
            slot = (1 << b) - 1 + j
            theirs = lax.rem(peer, 1 << b) * cnt
            out.append(remote(
                gout.at[b, pl.ds(pl.multiple_of(theirs, cnt), cnt), hcol(u)], gin.at[slot, pl.ds(0, cnt), hcol(u)],
                gs_s.at[u, slot], gs_r.at[u, slot], ctx=peer))
        return out

    dkp[...] = jnp.zeros_like(dkp)

    def back_level0(h, carry):
        hs = pl.ds(pl.multiple_of(h * HD, HD), HD)
        ks = kcol(h)
        vs = vcol(h)
        for b in range(blocks):
            br = slice(b * LEAF, (b + 1) * LEAF)
            kr = slice(b * LEAF, (b + 3) * LEAF)
            eb = e0[h, br]
            gb = g0[br, hs]
            keys = kp[kr, ks]
            d = d0[h, br]
            inner = nt(gb, kp[kr, vs])
            ds = (eb.astype(F32) * (inner - jnp.concatenate([d, d, d], axis=1))).astype(BF16)
            xc[br] = nn(ds, keys) * scale
            dkp[kr, ks] += tn(ds, q_ref[br, hs]) * scale
            dkp[kr, vs] += tn(eb, gb)
        for l in levels[: local - 1]:
            coarse_back(h, l)
        chain = None
        for l in reversed(levels):
            cnt = rows >> l
            x = dql[at(l) : at(l) + cnt, hs]
            if chain is not None:
                x = x + spread(xa, chain * 0.5, cnt // 2)
            chain = x
        dq_ref[:, hs] = (xc[...] + spread(xa, chain * 0.5, rows // 2)).astype(BF16)
        return carry

    def rim_left(u):
        return remote(rout.at[0, :, hcol(u)], rin.at[1, :, hcol(u)], rim_s.at[u, 0], rim_r.at[u, 1], ctx=left)

    def rim_right(u):
        return remote(rout.at[1, :, hcol(u)], rin.at[0, :, hcol(u)], rim_s.at[u, 1], rim_r.at[u, 0], ctx=right)

    twice = spread_matrix(LEAF, 0.5)

    def spread_wide(x, cnt):
        return nn(twice[: 2 * cnt, : cnt], x.astype(BF16))

    def send_grads(u):
        for b in range(cross):
            for c in grad_copies(u, b):
                c.start()

    def send_rims(u):
        rout[0, :, hcol(u)] = dkp[:LEAF, hcol(u)].astype(BF16)
        rout[1, :, hcol(u)] = dkp[LEAF + rows :, hcol(u)].astype(BF16)
        run_if(has_left, rim_left(u).start)
        run_if(has_right, rim_right(u).start)

    def finish(u):
        for b in range(cross):
            for c in grad_copies(u, b):
                c.wait()
        chain = None
        for b in reversed(range(cross)):
            cnt = LEAF >> b
            x = 0.0
            for j in range(1 << b):
                x = x + gin[(1 << b) - 1 + j, :cnt, hcol(u)].astype(F32)
            if chain is not None:
                x = x + spread_wide(chain, cnt // 2)
            chain = x
        dkv1[:, hcol(u)] += spread_wide(chain, LEAF)
        for b in range(blocks // 2):
            dkp[LEAF * (1 + 2 * b) : LEAF * (3 + 2 * b), hcol(u)] += spread_wide(
                dkv1[b * LEAF : (b + 1) * LEAF, hcol(u)], LEAF)

        def left_arrival():
            rim_right(u).wait_recv()
            dkp[LEAF : 2 * LEAF, hcol(u)] += rin[0, :, hcol(u)].astype(F32)

        def right_arrival():
            rim_left(u).wait_recv()
            dkp[rows : rows + LEAF, hcol(u)] += rin[1, :, hcol(u)].astype(F32)

        run_if(has_left, left_arrival)
        run_if(has_right, right_arrival)
        dk_ref[:, u * hw : (u + 1) * hw] = dkp[LEAF : LEAF + rows, u * 2 * hw : u * 2 * hw + hw].astype(BF16)
        dv_ref[:, u * hw : (u + 1) * hw] = dkp[LEAF : LEAF + rows, u * 2 * hw + hw : (u + 1) * 2 * hw].astype(BF16)

    chains = []

    def advance():
        for c in list(chains):
            if next(c, chains) is chains:
                chains.remove(c)

    for u in range(halves):
        take_kv(u)
        lax.fori_loop(u * per, (u + 1) * per, forward, 0)
        advance()
        chains.append(weight_grad(u))
        next(chains[-1])
        lax.fori_loop(u * per, (u + 1) * per, back_cross, 0)
        send_grads(u)
        advance()
    for u in range(halves):
        lax.fori_loop(u * per, (u + 1) * per, back_level0, 0)
        send_rims(u)
        advance()
    for u in range(halves):
        finish(u)
        advance()
    while chains:
        advance()
    wf_ref[...] = wfin[...]
    for u in range(halves):
        sent_kv(u)
        run_if(has_left, rim_left(u).wait_send)
        run_if(has_right, rim_right(u).wait_send)


def settle(dq_in, dk_in, dv_in, wf, dq, dk, dv, gw):
    dq[...] = dq_in[...]
    dk[...] = dk_in[...]
    dv[...] = dv_in[...]
    halves, cores, size, cols = wf.shape
    for u in range(halves):
        for c in range(cores):
            gw[u * size : (u + 1) * size, c * cols : (c + 1) * cols] = wf[u, c].astype(F32)


def body(queries, key_states, value_states, grad_out, out_weight):
    n = lax.axis_size("ctx")
    rows, wide = queries.shape[1:]
    heads = wide // HD
    cross = n.bit_length() - 1
    width = grad_out.shape[2]
    coarse = sum(rows >> l for l in range(1, (rows // LEAF).bit_length() - 1 + cross))
    halves = 2 if heads % 2 == 0 and wide // 2 // n >= 16 else 1
    hw = wide // halves
    cols = width // 2
    pieces = n - 1
    vm = pltpu.VMEM
    dma = pltpu.SemaphoreType.DMA
    scratch = [
        vm((rows + 2 * LEAF, 2 * wide), BF16),
        vm((rows // 2, 2 * wide), BF16),
        vm((cross, LEAF, 2 * wide), BF16),
        vm((coarse, wide), BF16),
        vm((rows, wide), BF16),
        vm((cross, LEAF, 2 * wide), BF16),
        vm((rows, wide), BF16),
        vm((heads, rows, 3 * LEAF), BF16),
        vm((rows, wide), BF16),
        vm((heads, rows, HD), F32),
        vm((heads, coarse, LEAF), BF16),
        vm((heads, coarse, HD), BF16),
        vm((heads, coarse, HD), F32),
        vm((coarse, HD), F32),
        vm((coarse, HD), F32),
        vm((rows, HD), F32),
        vm((rows, HD), F32),
        vm((rows, HD), F32),
        vm((rows + 2 * LEAF, 2 * wide), F32),
        vm((rows // 2, 2 * wide), F32),
        vm((cross, LEAF, 2 * wide), BF16),
        vm((pieces, LEAF, 2 * wide), BF16),
        vm((2, LEAF, 2 * wide), BF16),
        vm((2, LEAF, 2 * wide), BF16),
        vm((coarse, wide), F32),
        vm((halves, hw, width), F32),
        vm((halves, hw, cols), BF16),
        vm((halves, hw, cols), BF16),
        vm((halves, hw, cols), F32),
        vm((halves, hw, cols), BF16),
        vm((halves, hw, cols), BF16),
        vm((halves, 2, hw, cols), BF16),
        dma((halves, 2)), dma((halves, 2)),
        dma((halves, pieces)), dma((halves, pieces)),
        dma((halves, pieces)), dma((halves, pieces)),
        dma((halves, 2)), dma((halves, 2)),
        dma((halves,)), dma((halves,)),
        dma((halves, pieces)), dma((halves, pieces)),
        dma((halves, pieces)), dma((halves, pieces)),
        dma((halves,)), dma((halves,)),
    ]
    spec = pl.BlockSpec(memory_space=pltpu.VMEM)
    out = pl.pallas_call(
        functools.partial(kernel, n, heads, rows, halves),
        out_shape=[jax.ShapeDtypeStruct((rows, wide), BF16)] * 3
        + [jax.ShapeDtypeStruct((halves, 2, hw, cols), BF16)],
        in_specs=[spec] * 5,
        out_specs=[spec] * 4,
        scratch_shapes=scratch,
        compiler_params=pltpu.CompilerParams(
            collective_id=0, has_side_effects=True, vmem_limit_bytes=56 * 2**20
        ),
    )(queries[0], key_states[0], value_states[0], grad_out[0], out_weight)
    small = jax.ShapeDtypeStruct((rows, wide), BF16)
    dq, dk, dv, gw = pl.pallas_call(
        settle,
        out_shape=[small, small, small, jax.ShapeDtypeStruct((wide, width), F32)],
        in_specs=[spec] * 4,
        out_specs=[spec] * 4,
    )(*out)
    return dq[None], dk[None], dv[None], gw


def solution(mesh):
    row = P(("groups", "batch"), "ctx", "head")
    in_specs = (row, row, row, P(("groups", "batch"), "ctx", None), P("head", None))
    out_specs = (row, row, row, P(("groups", "head"), None))
    return jax.shard_map(body, mesh=mesh, in_specs=in_specs, out_specs=out_specs, check_vma=False)
```
